256 devices in a mesh: row: 16 (over x_lo, y, core), col: 16 (over x_hi, z).
Axes of the slice: x: 4 (x_hi: 2, x_lo: 2; x = x_hi * 2 + x_lo), y: 4, z: 8, core: 2. Of those that a mesh axis runs over, the one named last changes fastest.
Arguments:
- matrix: float32 [16384, 24576], P('col', 'row')
- inverse: float32 [256, 256], replicated, as said below
- pivots: int32 [256], replicated, may hold values from 256 to 16383, as said below
Outputs:
- factored: float32 [16384, 24576], P('col', 'row')
The draws below stay inside these ranges and needn't reach their ends.
Inputs may be any that keep to these rules, and one draw needn't show every extreme that they name: The 256 pivots are distinct and none lies among the top 256 rows. `inverse`: unit lower triangular.
All inputs are finite; a program needn't handle non-finite values.
Results may differ from the reference program's by a relative error of at most 0.0033.
Values may be sent and summed in bfloat16 or wider, within the bound.
A program may use at most 128 MiB of HBM per device.

```python
import jax
import jax.numpy as jnp
from jax import lax

NB = 256
MR = 16384
MC = 24576


def draw_matrix(key, part):
    key = jax.random.fold_in(key, 11)
    entries = jax.random.normal(key, (MR, MC), jnp.float32)
    column_scale = jnp.where(jnp.arange(MC) < NB, NB ** (-0.5), 1.0).astype(jnp.float32)
    return entries * column_scale[None, :]


def draw_inverse(key, part):
    key = jax.random.fold_in(key, 12)
    entries = jax.random.normal(key, (NB, NB), jnp.float32)
    return jnp.tril(entries * NB ** (-0.5), -1) + jnp.eye(NB, dtype=jnp.float32)


def draw_pivots(key, part):
    key = jax.random.fold_in(key, 13)
    key_one, key_two = jax.random.split(key)
    interior = jax.random.permutation(key_one, MR - NB - 2)[:NB - 2] + NB + 1
    values = jnp.concatenate([interior.astype(jnp.int32), jnp.array([NB, MR - 1], dtype=jnp.int32)])
    ordering = jax.random.permutation(key_two, NB)
    return values[ordering].astype(jnp.int32)


def setup_inputs(seed: int = 0) -> dict:
    seeds = jax.random.split(jax.random.key(seed), 4)
    return {
        "matrix": draw_matrix(jax.random.fold_in(seeds[3], 71), 0),
        "inverse": draw_inverse(jax.random.fold_in(seeds[3], 71), 0),
        "pivots": draw_pivots(jax.random.fold_in(seeds[3], 71), 0),
    }


def reference(matrix, inverse, pivots):
    trailing = matrix[:, NB:]
    pivot_block = trailing[pivots]
    former_top = trailing[:NB]
    upper_rows = jnp.dot(inverse, pivot_block, precision=lax.Precision.HIGHEST, preferred_element_type=jnp.float32)
    lower_rows = matrix[NB:, :NB].astype(jnp.bfloat16)
    product = jnp.dot(lower_rows, upper_rows.astype(jnp.bfloat16), preferred_element_type=jnp.float32)
    shifted = (pivots - NB).astype(jnp.int32)
    updated = trailing[NB:] - product
    updated = updated.at[shifted].set(former_top - product[shifted])
    result = jnp.concatenate([upper_rows, updated], axis=0)
    return jnp.concatenate([matrix[:, :NB], result], axis=1)
```

```python
import functools

import jax
import jax.numpy as jnp
from jax import lax
from jax.experimental import pallas as pl
from jax.experimental.pallas import tpu as pltpu
from jax.sharding import PartitionSpec as P

MESH = pl.DeviceIdType.MESH
NB = 256
CAP = 32
LANES = 128
Z = 8
COLS = 16
CHUNKS = 4
RING = 6


def from_root(array, axis, root):
    mine = lax.axis_index(axis) == root
    return lax.psum(jnp.where(mine, array, jnp.zeros_like(array)), axis)


def any_pivots(matrix, inverse, pivots):
    rows_dev, cols_dev = matrix.shape
    block_width = inverse.shape[0]
    grid_col = lax.axis_index("col")
    grid_row = lax.axis_index("row")
    local_rows = pivots - grid_col * rows_dev
    owned_here = (local_rows >= 0) & (local_rows < rows_dev)
    picked = jnp.take(matrix, jnp.clip(local_rows, 0, rows_dev - 1), axis=0)
    picked = jnp.where(owned_here[:, None], picked, 0.0)
    panel_rows = from_root(matrix[:, :block_width].astype(jnp.bfloat16), "row", 0)
    pivot_block = lax.psum(picked, "col")
    top_block = from_root(matrix[:block_width].astype(jnp.bfloat16), "col", 0).astype(jnp.float32)
    upper_rows = jnp.dot(
        inverse, pivot_block, precision=lax.Precision.HIGHEST, preferred_element_type=jnp.float32
    )
    target = jnp.where(owned_here, local_rows, rows_dev)
    swapped = matrix.at[target].set(top_block, mode="drop")
    product = jnp.dot(
        panel_rows, upper_rows.astype(jnp.bfloat16), preferred_element_type=jnp.float32
    )
    updated = swapped - product
    updated = updated.at[:block_width].set(
        jnp.where(grid_col == 0, upper_rows, updated[:block_width])
    )
    column_ids = grid_row * cols_dev + jnp.arange(cols_dev)
    return jnp.where((column_ids < block_width)[None, :], matrix, updated)


def update_kernel(
    mat_hbm, inv_ref, piv_ref, out_ref,
    picked, gathered, panel, upper, tops, top, perm, hits, idx_v, idx_s,
    load_sem, idx_sem, own_sem, sp_send, sp_recv, pan_send, pan_recv, top_send, top_recv,
    z_send, x_send, up_recv,
):
    rows, cols = out_ref.shape
    tiles = cols // LANES
    part = rows // CHUNKS
    r = lax.axis_index("row")
    c = lax.axis_index("col")
    xlo, y, core = r // 8, (r // 2) % 4, r % 2
    xhi, z = c // Z, c % Z

    def row_dev(xlo_, y_, core_):
        return ((xlo_ * 4 + y_) * 2 + core_, c)

    def col_dev(c_):
        return (r, c_)

    def owner_of(t):
        q = t % RING
        return (t // RING) * Z + (q + 1 + (q >= 3).astype(jnp.int32) + 2 * core) % Z

    zq = (z - 2 * core + Z) % Z
    is_owner = (zq != 0) & (zq != 4)
    my_tile = xhi * RING + jnp.maximum(zq - 1 - (zq > 4).astype(jnp.int32), 0)

    barrier = pltpu.get_barrier_semaphore()
    for k in range(1, COLS):
        pl.semaphore_signal(barrier, inc=1, device_id=col_dev((c + k) % COLS), device_id_type=MESH)
    for dev in (
        row_dev(xlo, y, 1 - core), row_dev(xlo, (y + 1) % 4, core),
        row_dev(xlo, (y + 3) % 4, core), row_dev(1 - xlo, y, core),
    ):
        pl.semaphore_signal(barrier, inc=1, device_id=dev, device_id_type=MESH)

    loads = [
        pltpu.make_async_copy(
            mat_hbm.at[pl.ds(k * part, part)], out_ref.at[pl.ds(k * part, part)], load_sem.at[k]
        )
        for k in range(CHUNKS)
    ]
    for load in loads:
        load.start()

    i_id = lax.broadcasted_iota(jnp.int32, (NB, NB), 0)
    j_id = lax.broadcasted_iota(jnp.int32, (NB, NB), 1)
    piv_row = jnp.broadcast_to(piv_ref[...], (NB, NB))
    piv_col = piv_row.T
    own_row, own_col = piv_row // rows, piv_col // rows
    rank = jnp.sum(((own_row == own_col) & (i_id < j_id)).astype(jnp.int32), axis=0, keepdims=True)
    slot_row = jnp.broadcast_to(own_row[:1] * CAP + rank, (NB, NB))
    slot_col = slot_row.T
    lane = j_id[:, :LANES]
    match = (slot_col[:, :LANES] == c * CAP + lane) & (lane < CAP)
    idx = jnp.sum(
        jnp.where(match, piv_col[:, :LANES] - c * rows + 1, 0), axis=0, keepdims=True
    ) - 1
    idx_v[...] = jnp.maximum(idx, 0)
    idx_copy = pltpu.make_async_copy(idx_v, idx_s, idx_sem)
    idx_copy.start()
    r_id = lax.broadcasted_iota(jnp.int32, (rows, LANES), 0)
    hits[...] = (r_id == jnp.broadcast_to(idx, (rows, LANES))).astype(jnp.float32).astype(jnp.bfloat16)
    top[CAP:, :] = jnp.zeros((LANES - CAP, cols), jnp.bfloat16)
    idx_copy.wait()
    for load in loads:
        load.wait()

    for k in range(CAP):
        row = out_ref[pl.ds(idx_s[0, k], 1), :]
        for t in range(tiles):
            picked[t, k : k + 1, :] = row[:, t * LANES : (t + 1) * LANES]

    pl.semaphore_wait(barrier, COLS - 1 + 4)

    def pick_copy(t):
        return pltpu.make_async_remote_copy(
            src_ref=picked.at[t], dst_ref=gathered.at[c], send_sem=sp_send.at[t],
            recv_sem=sp_recv.at[c], device_id=col_dev(owner_of(t)), device_id_type=MESH,
        )

    def for_tiles(body):
        lax.fori_loop(0, tiles, lambda t, _: (body(t), 0)[1], 0)

    @for_tiles
    def _(t):
        @pl.when(owner_of(t) != c)
        def _():
            pick_copy(t).start()

    def pan_copy(k, child, dev):
        return pltpu.make_async_remote_copy(
            src_ref=panel.at[k], dst_ref=panel.at[k], send_sem=pan_send.at[k, child],
            recv_sem=pan_recv.at[k], device_id=dev, device_id_type=MESH,
        )

    def pan_children(k):
        return [
            ((core == 0) & (y == 0), row_dev(xlo, 1, 0)),
            ((core == 0) & (y == 0), row_dev(xlo, 3, 0)),
            ((core == 0) & (y == 0) & (xlo == 0), row_dev(1, 0, 0)),
            ((core == 0) & (y == (1 if k < CHUNKS // 2 else 3)), row_dev(xlo, 2, 0)),
            (core == 0, row_dev(xlo, y, 1)),
        ]

    def pan_forward(k):
        for child, (cond, dev) in enumerate(pan_children(k)):
            @pl.when(cond)
            def _():
                pan_copy(k, child, dev).start()

    def pan_wait(k):
        pan_copy(k, 0, row_dev(xlo, y, 1 - core)).wait_recv()

    @pl.when(r == 0)
    def _():
        for k in range(CHUNKS):
            panel[k] = out_ref[k * part : (k + 1) * part, :NB].astype(jnp.bfloat16)
            pan_forward(k)

    def top_copy(dst):
        return pltpu.make_async_remote_copy(
            src_ref=tops.at[dst], dst_ref=top.at[pl.ds(0, CAP)], send_sem=top_send.at[dst],
            recv_sem=top_recv, device_id=col_dev(dst), device_id_type=MESH,
        )

    @pl.when(c == 0)
    def _():
        s_id = lax.broadcasted_iota(jnp.int32, (NB, NB), 0)
        block = out_ref[:NB, :].astype(jnp.bfloat16)
        half = NB // CAP
        for h in range(COLS * CAP // NB):
            pick = (slot_row == s_id + h * NB).astype(jnp.float32).astype(jnp.bfloat16)
            sent = jnp.dot(pick, block, preferred_element_type=jnp.float32).astype(jnp.bfloat16)
            tops[h * half : (h + 1) * half] = sent.reshape(half, CAP, cols)
            for dst in range(max(1, h * half), (h + 1) * half):
                top_copy(dst).start()
        pltpu.make_async_copy(tops.at[0], top.at[pl.ds(0, CAP)], own_sem).start()

    for h in range(COLS * CAP // NB):
        place = (slot_col == j_id + h * NB).astype(jnp.float32)
        perm[:, h * NB : (h + 1) * NB] = jnp.dot(
            inv_ref[...], place, precision=lax.Precision.HIGHEST, preferred_element_type=jnp.float32
        )

    depth_one = (core == 0) & (((xlo == 0) & ((y == 1) | (y == 3))) | ((xlo == 1) & (y == 0)))

    @pl.when(depth_one)
    def _():
        for k in range(CHUNKS):
            pan_wait(k)
            pan_forward(k)

    def z_copy(k):
        return pltpu.make_async_remote_copy(
            src_ref=upper.at[my_tile], dst_ref=upper.at[my_tile], send_sem=z_send.at[k],
            recv_sem=up_recv.at[my_tile], device_id=col_dev(xhi * Z + (z + k) % Z), device_id_type=MESH,
        )

    def x_copy(t):
        return pltpu.make_async_remote_copy(
            src_ref=upper.at[t], dst_ref=upper.at[t], send_sem=x_send.at[t],
            recv_sem=up_recv.at[t], device_id=col_dev((1 - xhi) * Z + z), device_id_type=MESH,
        )

    @pl.when(is_owner)
    def _():
        gathered[c] = picked[my_tile]
        for k in range(1, COLS):
            src = (c + k) % COLS
            pltpu.make_async_remote_copy(
                src_ref=picked.at[0], dst_ref=gathered.at[src], send_sem=sp_send.at[0],
                recv_sem=sp_recv.at[src], device_id=col_dev(src), device_id_type=MESH,
            ).wait_recv()
        solved = jnp.dot(
            perm[...], gathered[...].reshape(COLS * CAP, LANES),
            precision=lax.Precision.HIGHEST, preferred_element_type=jnp.float32,
        )
        upper[my_tile] = solved.astype(jnp.bfloat16)
        for k in (4, 3, 5, 2, 6, 1, 7):
            z_copy(k).start()
        x_copy(my_tile).start()

    @pl.when(jnp.logical_not(depth_one) & (r != 0))
    def _():
        for k in range(CHUNKS):
            pan_wait(k)
            pan_forward(k)

    first = xhi * RING
    for q in range(RING):
        @pl.when((first + q != my_tile) | jnp.logical_not(is_owner))
        def _():
            x_copy(first + q).wait_recv()
            x_copy(first + q).start()

    @pl.when(c == 0)
    def _():
        pltpu.make_async_copy(tops.at[0], top.at[pl.ds(0, CAP)], own_sem).wait()

    @pl.when(c != 0)
    def _():
        top_copy(c).wait_recv()

    def trailing(t):
        return (r != 0) | (t >= NB // LANES)

    def columns(t):
        return pl.ds(pl.multiple_of(t * LANES, LANES), LANES)

    taken = jnp.sum(hits[...].astype(jnp.float32), axis=1, keepdims=True) > 0.5

    @for_tiles
    def _(t):
        @pl.when(trailing(t))
        def _():
            moved = jnp.dot(hits[...], top[:, columns(t)], preferred_element_type=jnp.float32)
            out_ref[:, columns(t)] = jnp.where(taken, moved, out_ref[:, columns(t)])

    def apply(t):
        @pl.when(trailing(t))
        def _():
            for k in range(CHUNKS):
                rows_k = pl.ds(k * part, part)
                out_ref[rows_k, columns(t)] = out_ref[rows_k, columns(t)] - jnp.dot(
                    panel[k], upper[t], preferred_element_type=jnp.float32
                )

            @pl.when(c == 0)
            def _():
                out_ref[:NB, columns(t)] = upper[t].astype(jnp.float32)

    def loop(body):
        lax.fori_loop(0, RING, lambda q, _: (body(q), 0)[1], 0)

    @loop
    def _(q):
        apply(first + q)

    @loop
    def _(q):
        t = (1 - xhi) * RING + q
        x_copy(t).wait_recv()
        apply(t)

    @for_tiles
    def _(t):
        @pl.when(owner_of(t) != c)
        def _():
            pick_copy(t).wait_send()

    for k in range(CHUNKS):
        for child, (cond, dev) in enumerate(pan_children(k)):
            @pl.when(cond)
            def _():
                pan_copy(k, child, dev).wait_send()

    @pl.when(c == 0)
    def _():
        for dst in range(1, COLS):
            top_copy(dst).wait_send()

    @pl.when(is_owner)
    def _():
        for k in range(1, Z):
            z_copy(k).wait_send()

    for q in range(RING):
        x_copy(first + q).wait_send()


def store_kernel(src, dst, sems):
    part = src.shape[0] // CHUNKS
    copies = [
        pltpu.make_async_copy(
            src.at[pl.ds(k * part, part)], dst.at[pl.ds(k * part, part)], sems.at[k]
        )
        for k in range(CHUNKS)
    ]
    for copy in copies:
        copy.start()
    for copy in copies:
        copy.wait()


def store(block):
    return pl.pallas_call(
        store_kernel,
        out_shape=jax.ShapeDtypeStruct(block.shape, block.dtype),
        in_specs=[pl.BlockSpec(memory_space=pltpu.VMEM)],
        out_specs=pl.BlockSpec(memory_space=pltpu.HBM),
        scratch_shapes=[pltpu.SemaphoreType.DMA((CHUNKS,))],
        compiler_params=pltpu.CompilerParams(vmem_limit_bytes=1 << 20),
        name="store",
    )(block)


def fast_update(matrix, inverse, pivots):
    rows, cols = matrix.shape
    tiles = cols // LANES
    dma = pltpu.SemaphoreType.DMA
    updated = pl.pallas_call(
        update_kernel,
        out_shape=pltpu.VMEM((rows, cols), jnp.float32),
        in_specs=[
            pl.BlockSpec(memory_space=pltpu.HBM),
            pl.BlockSpec(memory_space=pltpu.VMEM),
            pl.BlockSpec(memory_space=pltpu.VMEM),
        ],
        out_specs=pl.BlockSpec(memory_space=pltpu.VMEM),
        scratch_shapes=[
            pltpu.VMEM((tiles, CAP, LANES), jnp.float32),
            pltpu.VMEM((COLS, CAP, LANES), jnp.float32),
            pltpu.VMEM((CHUNKS, rows // CHUNKS, NB), jnp.bfloat16),
            pltpu.VMEM((tiles, NB, LANES), jnp.bfloat16),
            pltpu.VMEM((COLS, CAP, cols), jnp.bfloat16),
            pltpu.VMEM((LANES, cols), jnp.bfloat16),
            pltpu.VMEM((NB, COLS * CAP), jnp.float32),
            pltpu.VMEM((rows, LANES), jnp.bfloat16),
            pltpu.VMEM((1, LANES), jnp.int32),
            pltpu.SMEM((1, LANES), jnp.int32),
            dma((CHUNKS,)), dma, dma, dma((tiles,)), dma((COLS,)),
            dma((CHUNKS, 5)), dma((CHUNKS,)), dma((COLS,)), dma,
            dma((Z,)), dma((tiles,)), dma((tiles,)),
        ],
        compiler_params=pltpu.CompilerParams(
            collective_id=0, has_side_effects=True, vmem_limit_bytes=16 << 20
        ),
        name="update",
    )(matrix, inverse, pivots.reshape(1, NB))
    return store(updated)


def per_device(matrix, inverse, pivots):
    rows = matrix.shape[0]
    held = jnp.sum((pivots[:, None] // rows == jnp.arange(COLS)[None, :]).astype(jnp.int32), axis=0)
    fits = jnp.max(held) <= CAP
    return lax.cond(fits, fast_update, any_pivots, matrix, inverse, pivots)


def solution(mesh):
    return jax.shard_map(
        per_device,
        mesh=mesh,
        in_specs=(P("col", "row"), P(), P()),
        out_specs=P("col", "row"),
        check_vma=False,
    )
```

```python
import functools

import jax
import jax.numpy as jnp
from jax import lax
from jax.experimental import pallas as pl
from jax.experimental.pallas import tpu as pltpu
from jax.sharding import PartitionSpec as P

MESH = pl.DeviceIdType.MESH
NB = 256
CAP = 32
LANES = 128
Z = 8
COLS = 16
CHUNKS = 4
RING = 6


def total(array, axis):
    for step in (1, 2, 4, 8):
        array = array + lax.ppermute(array, axis, [(i, i ^ step) for i in range(COLS)])
    return array


def from_root(array, axis, root):
    mine = lax.axis_index(axis) == root
    return total(jnp.where(mine, array, jnp.zeros_like(array)), axis)


def any_pivots(matrix, inverse, pivots):
    rows_dev, cols_dev = matrix.shape
    block_width = inverse.shape[0]
    grid_col = lax.axis_index("col")
    grid_row = lax.axis_index("row")
    local_rows = pivots - grid_col * rows_dev
    owned_here = (local_rows >= 0) & (local_rows < rows_dev)
    picked = jnp.take(matrix, jnp.clip(local_rows, 0, rows_dev - 1), axis=0)
    picked = jnp.where(owned_here[:, None], picked, 0.0)
    panel_rows = from_root(matrix[:, :block_width].astype(jnp.bfloat16), "row", 0)
    pivot_block = total(picked, "col")
    top_block = from_root(matrix[:block_width].astype(jnp.bfloat16), "col", 0).astype(jnp.float32)
    upper_rows = jnp.dot(
        inverse, pivot_block, precision=lax.Precision.HIGHEST, preferred_element_type=jnp.float32
    )
    row_ids = jnp.arange(rows_dev)
    hit = row_ids[:, None] == local_rows[None, :]
    source = jnp.sum(jnp.where(hit, jnp.arange(block_width)[None, :], 0), axis=1)
    moved = jnp.take(top_block, source, axis=0)
    swapped = jnp.where(jnp.any(hit, axis=1)[:, None], moved, matrix)
    product = jnp.dot(
        panel_rows, upper_rows.astype(jnp.bfloat16), preferred_element_type=jnp.float32
    )
    updated = swapped - product
    solved = jnp.concatenate([upper_rows, jnp.zeros_like(updated[block_width:])], axis=0)
    updated = jnp.where(((grid_col == 0) & (row_ids < block_width))[:, None], solved, updated)
    column_ids = grid_row * cols_dev + jnp.arange(cols_dev)
    return jnp.where((column_ids < block_width)[None, :], matrix, updated)


def update_kernel(
    mat_hbm, inv_ref, piv_ref, out_ref,
    picked, gathered, panel, upper, tops, top, perm, hits, idx_v, idx_s,
    load_sem, idx_sem, own_sem, sp_send, sp_recv, pan_send, pan_recv, top_send, top_recv,
    z_send, x_send, up_recv,
):
    rows, cols = out_ref.shape
    tiles = cols // LANES
    part = rows // CHUNKS
    r = lax.axis_index("row")
    c = lax.axis_index("col")
    xlo, y, core = r // 8, (r // 2) % 4, r % 2
    xhi, z = c // Z, c % Z

    def row_dev(xlo_, y_, core_):
        return ((xlo_ * 4 + y_) * 2 + core_, c)

    def col_dev(c_):
        return (r, c_)

    def owner_of(t):
        q = t % RING
        return (t // RING) * Z + (q + 1 + (q >= 3).astype(jnp.int32) + 2 * core) % Z

    zq = (z - 2 * core + Z) % Z
    is_owner = (zq != 0) & (zq != 4)
    my_tile = xhi * RING + jnp.maximum(zq - 1 - (zq > 4).astype(jnp.int32), 0)

    barrier = pltpu.get_barrier_semaphore()
    for k in range(1, COLS):
        pl.semaphore_signal(barrier, inc=1, device_id=col_dev((c + k) % COLS), device_id_type=MESH)
    for dev in (
        row_dev(xlo, y, 1 - core), row_dev(xlo, (y + 1) % 4, core),
        row_dev(xlo, (y + 3) % 4, core), row_dev(1 - xlo, y, core),
    ):
        pl.semaphore_signal(barrier, inc=1, device_id=dev, device_id_type=MESH)

    loads = [
        pltpu.make_async_copy(
            mat_hbm.at[pl.ds(k * part, part)], out_ref.at[pl.ds(k * part, part)], load_sem.at[k]
        )
        for k in range(CHUNKS)
    ]
    for load in loads:
        load.start()

    i_id = lax.broadcasted_iota(jnp.int32, (NB, NB), 0)
    j_id = lax.broadcasted_iota(jnp.int32, (NB, NB), 1)
    piv_row = jnp.broadcast_to(piv_ref[...], (NB, NB))
    piv_col = piv_row.T
    own_row, own_col = piv_row // rows, piv_col // rows
    rank = jnp.sum(((own_row == own_col) & (i_id < j_id)).astype(jnp.int32), axis=0, keepdims=True)
    slot_row = jnp.broadcast_to(own_row[:1] * CAP + rank, (NB, NB))
    slot_col = slot_row.T
    lane = j_id[:, :LANES]
    match = (slot_col[:, :LANES] == c * CAP + lane) & (lane < CAP)
    idx = jnp.sum(
        jnp.where(match, piv_col[:, :LANES] - c * rows + 1, 0), axis=0, keepdims=True
    ) - 1
    idx_v[...] = jnp.maximum(idx, 0)
    idx_copy = pltpu.make_async_copy(idx_v, idx_s, idx_sem)
    idx_copy.start()
    r_id = lax.broadcasted_iota(jnp.int32, (rows, LANES), 0)
    hits[...] = (r_id == jnp.broadcast_to(idx, (rows, LANES))).astype(jnp.float32).astype(jnp.bfloat16)
    top[CAP:, :] = jnp.zeros((LANES - CAP, cols), jnp.bfloat16)
    idx_copy.wait()
    for load in loads:
        load.wait()

    for k in range(CAP):
        row = out_ref[pl.ds(idx_s[0, k], 1), :]
        for t in range(tiles):
            picked[t, k : k + 1, :] = row[:, t * LANES : (t + 1) * LANES]

    pl.semaphore_wait(barrier, COLS - 1 + 4)

    def pick_copy(t):
        return pltpu.make_async_remote_copy(
            src_ref=picked.at[t], dst_ref=gathered.at[c], send_sem=sp_send.at[t],
            recv_sem=sp_recv.at[c], device_id=col_dev(owner_of(t)), device_id_type=MESH,
        )

    def for_tiles(body):
        lax.fori_loop(0, tiles, lambda t, _: (body(t), 0)[1], 0)

    @for_tiles
    def _(t):
        @pl.when(owner_of(t) != c)
        def _():
            pick_copy(t).start()

    def pan_copy(k, child, dev):
        return pltpu.make_async_remote_copy(
            src_ref=panel.at[k], dst_ref=panel.at[k], send_sem=pan_send.at[k, child],
            recv_sem=pan_recv.at[k], device_id=dev, device_id_type=MESH,
        )

    def pan_children(k):
        return [
            ((core == 0) & (y == 0), row_dev(xlo, 1, 0)),
            ((core == 0) & (y == 0), row_dev(xlo, 3, 0)),
            ((core == 0) & (y == 0) & (xlo == 0), row_dev(1, 0, 0)),
            ((core == 0) & (y == (1 if k < CHUNKS // 2 else 3)), row_dev(xlo, 2, 0)),
            (core == 0, row_dev(xlo, y, 1)),
        ]

    def pan_forward(k):
        for child, (cond, dev) in enumerate(pan_children(k)):
            @pl.when(cond)
            def _():
                pan_copy(k, child, dev).start()

    def pan_wait(k):
        pan_copy(k, 0, row_dev(xlo, y, 1 - core)).wait_recv()

    @pl.when(r == 0)
    def _():
        for k in range(CHUNKS):
            panel[k] = out_ref[k * part : (k + 1) * part, :NB].astype(jnp.bfloat16)
            pan_forward(k)

    def top_copy(dst):
        return pltpu.make_async_remote_copy(
            src_ref=tops.at[dst], dst_ref=top.at[pl.ds(0, CAP)], send_sem=top_send.at[dst],
            recv_sem=top_recv, device_id=col_dev(dst), device_id_type=MESH,
        )

    @pl.when(c == 0)
    def _():
        s_id = lax.broadcasted_iota(jnp.int32, (NB, NB), 0)
        block = out_ref[:NB, :].astype(jnp.bfloat16)
        half = NB // CAP
        for h in range(COLS * CAP // NB):
            pick = (slot_row == s_id + h * NB).astype(jnp.float32).astype(jnp.bfloat16)
            sent = jnp.dot(pick, block, preferred_element_type=jnp.float32).astype(jnp.bfloat16)
            tops[h * half : (h + 1) * half] = sent.reshape(half, CAP, cols)
            for dst in range(max(1, h * half), (h + 1) * half):
                top_copy(dst).start()
        pltpu.make_async_copy(tops.at[0], top.at[pl.ds(0, CAP)], own_sem).start()

    for h in range(COLS * CAP // NB):
        place = (slot_col == j_id + h * NB).astype(jnp.float32)
        perm[:, h * NB : (h + 1) * NB] = jnp.dot(
            inv_ref[...], place, precision=lax.Precision.HIGHEST, preferred_element_type=jnp.float32
        )

    depth_one = (core == 0) & (((xlo == 0) & ((y == 1) | (y == 3))) | ((xlo == 1) & (y == 0)))

    @pl.when(depth_one)
    def _():
        for k in range(CHUNKS):
            pan_wait(k)
            pan_forward(k)

    def z_copy(k):
        return pltpu.make_async_remote_copy(
            src_ref=upper.at[my_tile], dst_ref=upper.at[my_tile], send_sem=z_send.at[k],
            recv_sem=up_recv.at[my_tile], device_id=col_dev(xhi * Z + (z + k) % Z), device_id_type=MESH,
        )

    def x_copy(t):
        return pltpu.make_async_remote_copy(
            src_ref=upper.at[t], dst_ref=upper.at[t], send_sem=x_send.at[t],
            recv_sem=up_recv.at[t], device_id=col_dev((1 - xhi) * Z + z), device_id_type=MESH,
        )

    @pl.when(is_owner)
    def _():
        gathered[c] = picked[my_tile]
        for k in range(1, COLS):
            src = (c + k) % COLS
            pltpu.make_async_remote_copy(
                src_ref=picked.at[0], dst_ref=gathered.at[src], send_sem=sp_send.at[0],
                recv_sem=sp_recv.at[src], device_id=col_dev(src), device_id_type=MESH,
            ).wait_recv()
        solved = jnp.dot(
            perm[...], gathered[...].reshape(COLS * CAP, LANES),
            precision=lax.Precision.HIGHEST, preferred_element_type=jnp.float32,
        )
        upper[my_tile] = solved.astype(jnp.bfloat16)
        for k in (4, 3, 5, 2, 6, 1, 7):
            z_copy(k).start()
        x_copy(my_tile).start()

    @pl.when(jnp.logical_not(depth_one) & (r != 0))
    def _():
        for k in range(CHUNKS):
            pan_wait(k)
            pan_forward(k)

    first = xhi * RING
    for q in range(RING):
        @pl.when((first + q != my_tile) | jnp.logical_not(is_owner))
        def _():
            x_copy(first + q).wait_recv()
            x_copy(first + q).start()

    @pl.when(c == 0)
    def _():
        pltpu.make_async_copy(tops.at[0], top.at[pl.ds(0, CAP)], own_sem).wait()

    @pl.when(c != 0)
    def _():
        top_copy(c).wait_recv()

    def trailing(t):
        return (r != 0) | (t >= NB // LANES)

    def columns(t):
        return pl.ds(pl.multiple_of(t * LANES, LANES), LANES)

    taken = jnp.sum(hits[...].astype(jnp.float32), axis=1, keepdims=True) > 0.5

    @for_tiles
    def _(t):
        @pl.when(trailing(t))
        def _():
            moved = jnp.dot(hits[...], top[:, columns(t)], preferred_element_type=jnp.float32)
            out_ref[:, columns(t)] = jnp.where(taken, moved, out_ref[:, columns(t)])

    def apply(t):
        @pl.when(trailing(t))
        def _():
            for k in range(CHUNKS):
                rows_k = pl.ds(k * part, part)
                out_ref[rows_k, columns(t)] = out_ref[rows_k, columns(t)] - jnp.dot(
                    panel[k], upper[t], preferred_element_type=jnp.float32
                )

            @pl.when(c == 0)
            def _():
                out_ref[:NB, columns(t)] = upper[t].astype(jnp.float32)

    def loop(body):
        lax.fori_loop(0, RING, lambda q, _: (body(q), 0)[1], 0)

    @loop
    def _(q):
        apply(first + q)

    @loop
    def _(q):
        t = (1 - xhi) * RING + q
        x_copy(t).wait_recv()
        apply(t)

    @for_tiles
    def _(t):
        @pl.when(owner_of(t) != c)
        def _():
            pick_copy(t).wait_send()

    for k in range(CHUNKS):
        for child, (cond, dev) in enumerate(pan_children(k)):
            @pl.when(cond)
            def _():
                pan_copy(k, child, dev).wait_send()

    @pl.when(c == 0)
    def _():
        for dst in range(1, COLS):
            top_copy(dst).wait_send()

    @pl.when(is_owner)
    def _():
        for k in range(1, Z):
            z_copy(k).wait_send()

    for q in range(RING):
        x_copy(first + q).wait_send()


def store_kernel(src, dst, sems):
    part = src.shape[0] // CHUNKS
    copies = [
        pltpu.make_async_copy(
            src.at[pl.ds(k * part, part)], dst.at[pl.ds(k * part, part)], sems.at[k]
        )
        for k in range(CHUNKS)
    ]
    for copy in copies:
        copy.start()
    for copy in copies:
        copy.wait()


def store(block):
    return pl.pallas_call(
        store_kernel,
        out_shape=jax.ShapeDtypeStruct(block.shape, block.dtype),
        in_specs=[pl.BlockSpec(memory_space=pltpu.VMEM)],
        out_specs=pl.BlockSpec(memory_space=pltpu.HBM),
        scratch_shapes=[pltpu.SemaphoreType.DMA((CHUNKS,))],
        compiler_params=pltpu.CompilerParams(vmem_limit_bytes=1 << 20),
        name="store",
    )(block)


def fast_update(matrix, inverse, pivots):
    rows, cols = matrix.shape
    tiles = cols // LANES
    dma = pltpu.SemaphoreType.DMA
    updated = pl.pallas_call(
        update_kernel,
        out_shape=pltpu.VMEM((rows, cols), jnp.float32),
        in_specs=[
            pl.BlockSpec(memory_space=pltpu.HBM),
            pl.BlockSpec(memory_space=pltpu.VMEM),
            pl.BlockSpec(memory_space=pltpu.VMEM),
        ],
        out_specs=pl.BlockSpec(memory_space=pltpu.VMEM),
        scratch_shapes=[
            pltpu.VMEM((tiles, CAP, LANES), jnp.float32),
            pltpu.VMEM((COLS, CAP, LANES), jnp.float32),
            pltpu.VMEM((CHUNKS, rows // CHUNKS, NB), jnp.bfloat16),
            pltpu.VMEM((tiles, NB, LANES), jnp.bfloat16),
            pltpu.VMEM((COLS, CAP, cols), jnp.bfloat16),
            pltpu.VMEM((LANES, cols), jnp.bfloat16),
            pltpu.VMEM((NB, COLS * CAP), jnp.float32),
            pltpu.VMEM((rows, LANES), jnp.bfloat16),
            pltpu.VMEM((1, LANES), jnp.int32),
            pltpu.SMEM((1, LANES), jnp.int32),
            dma((CHUNKS,)), dma, dma, dma((tiles,)), dma((COLS,)),
            dma((CHUNKS, 5)), dma((CHUNKS,)), dma((COLS,)), dma,
            dma((Z,)), dma((tiles,)), dma((tiles,)),
        ],
        compiler_params=pltpu.CompilerParams(
            collective_id=0, has_side_effects=True, vmem_limit_bytes=16 << 20
        ),
        name="update",
    )(matrix, inverse, pivots.reshape(1, NB))
    return store(updated)


def per_device(matrix, inverse, pivots):
    rows = matrix.shape[0]
    held = jnp.sum((pivots[:, None] // rows == jnp.arange(COLS)[None, :]).astype(jnp.int32), axis=0)
    fits = jnp.max(held) <= CAP
    return lax.cond(fits, fast_update, any_pivots, matrix, inverse, pivots)


def solution(mesh):
    return jax.shard_map(
        per_device,
        mesh=mesh,
        in_specs=(P("col", "row"), P(), P()),
        out_specs=P("col", "row"),
        check_vma=False,
    )
```

```python
import functools

import jax
import jax.numpy as jnp
from jax import lax
from jax.experimental import pallas as pl
from jax.experimental.pallas import tpu as pltpu
from jax.sharding import PartitionSpec as P

MESH = pl.DeviceIdType.MESH
NB = 256
CAP = 32
LANES = 128
Z = 8
COLS = 16
CHUNKS = 4
RING = 6
DIRECT = (2, 6, 1, 7)
RELAYED = (11, 10, 9)
TOP_ORDER = (12, 4, 11, 3, 14, 13, 5, 10, 2, 15, 6, 9, 1, 7, 8)


def total(array, axis):
    for step in (1, 2, 4, 8):
        array = array + lax.ppermute(array, axis, [(i, i ^ step) for i in range(COLS)])
    return array


def from_root(array, axis, root):
    mine = lax.axis_index(axis) == root
    return total(jnp.where(mine, array, jnp.zeros_like(array)), axis)


def any_pivots(matrix, inverse, pivots):
    rows_dev, cols_dev = matrix.shape
    block_width = inverse.shape[0]
    grid_col = lax.axis_index("col")
    grid_row = lax.axis_index("row")
    local_rows = pivots - grid_col * rows_dev
    owned_here = (local_rows >= 0) & (local_rows < rows_dev)
    picked = jnp.take(matrix, jnp.clip(local_rows, 0, rows_dev - 1), axis=0)
    picked = jnp.where(owned_here[:, None], picked, 0.0)
    panel_rows = from_root(matrix[:, :block_width].astype(jnp.bfloat16), "row", 0)
    pivot_block = total(picked, "col")
    top_block = from_root(matrix[:block_width].astype(jnp.bfloat16), "col", 0).astype(jnp.float32)
    upper_rows = jnp.dot(
        inverse, pivot_block, precision=lax.Precision.HIGHEST, preferred_element_type=jnp.float32
    )
    row_ids = jnp.arange(rows_dev)
    hit = row_ids[:, None] == local_rows[None, :]
    source = jnp.sum(jnp.where(hit, jnp.arange(block_width)[None, :], 0), axis=1)
    moved = jnp.take(top_block, source, axis=0)
    swapped = jnp.where(jnp.any(hit, axis=1)[:, None], moved, matrix)
    product = jnp.dot(
        panel_rows, upper_rows.astype(jnp.bfloat16), preferred_element_type=jnp.float32
    )
    updated = swapped - product
    solved = jnp.concatenate([upper_rows, jnp.zeros_like(updated[block_width:])], axis=0)
    updated = jnp.where(((grid_col == 0) & (row_ids < block_width))[:, None], solved, updated)
    column_ids = grid_row * cols_dev + jnp.arange(cols_dev)
    return jnp.where((column_ids < block_width)[None, :], matrix, updated)


def update_kernel(
    mat_hbm, inv_ref, piv_ref, out_ref, most_ref,
    picked, gathered, panel, upper, tops, top, perm, hits, idx_v, idx_s,
    load_sem, idx_sem, own_sem, sp_send, sp_recv, pan_send, pan_recv, top_send, top_recv,
    z_send, f_send, x_send, up_recv, half_recv, hand, hand_send, hand_recv, mask,
):
    rows, cols = out_ref.shape
    tiles = cols // LANES
    part = rows // CHUNKS
    r = lax.axis_index("row")
    c = lax.axis_index("col")
    xlo, y, core = r // 8, (r // 2) % 4, r % 2
    xhi, z = c // Z, c % Z

    def row_dev(xlo_, y_, core_):
        return ((xlo_ * 4 + y_) * 2 + core_, c)

    def col_dev(c_):
        return (r, c_)

    def owner_of(t):
        q = t % RING
        return (t // RING) * Z + q + 1 + (q >= 3).astype(jnp.int32)

    def tile_of(away):
        zq = (z + away + Z) % Z
        return xhi * RING + jnp.maximum(zq - 1 - (zq > 4).astype(jnp.int32), 0), zq % 4 != 0

    my_tile, is_owner = tile_of(0)

    loads = [
        pltpu.make_async_copy(
            mat_hbm.at[pl.ds(k * part, part)], out_ref.at[pl.ds(k * part, part)], load_sem.at[k]
        )
        for k in range(CHUNKS)
    ]
    for load in loads:
        load.start()

    barrier = pltpu.get_barrier_semaphore()
    for k in range(1, COLS):
        pl.semaphore_signal(barrier, inc=1, device_id=col_dev((c + k) % COLS), device_id_type=MESH)
    for dev in (
        row_dev(xlo, y, 1 - core), row_dev(xlo, (y + 1) % 4, core),
        row_dev(xlo, (y + 2) % 4, core), row_dev(xlo, (y + 3) % 4, core), row_dev(1 - xlo, y, core),
        row_dev(xlo, (y + 1) % 4, 1 - core), row_dev(xlo, (y + 3) % 4, 1 - core), row_dev(1 - xlo, y, 1 - core),
    ):
        pl.semaphore_signal(barrier, inc=1, device_id=dev, device_id_type=MESH)

    i_id = lax.broadcasted_iota(jnp.int32, (NB, NB), 0)
    j_id = lax.broadcasted_iota(jnp.int32, (NB, NB), 1)
    piv_row = jnp.broadcast_to(piv_ref[...], (NB, NB))
    piv_col = piv_row.T
    own_row, own_col = piv_row // rows, piv_col // rows
    rank = jnp.sum(((own_row == own_col) & (i_id < j_id)).astype(jnp.int32), axis=0, keepdims=True)
    most_ref[0, 0] = jnp.max(rank)
    slot = jnp.where(rank < CAP, own_row[:1] * CAP + rank, -1)
    slot_row = jnp.broadcast_to(slot, (NB, NB))
    slot_col = slot_row.T
    lane = j_id[:, :LANES]
    match = (slot_col[:, :LANES] == c * CAP + lane) & (lane < CAP)
    idx = jnp.sum(
        jnp.where(match, piv_col[:, :LANES] - c * rows + 1, 0), axis=0, keepdims=True
    ) - 1
    idx_v[...] = jnp.maximum(idx, 0)
    idx_copy = pltpu.make_async_copy(idx_v, idx_s, idx_sem)
    idx_copy.start()
    r_id = lax.broadcasted_iota(jnp.int32, (rows, LANES), 0)
    hits[...] = (r_id == jnp.broadcast_to(idx, (rows, LANES))).astype(jnp.float32).astype(jnp.bfloat16)
    top[CAP:, :] = jnp.zeros((LANES - CAP, cols), jnp.bfloat16)
    idx_copy.wait()
    for load in loads:
        load.wait()

    for k in range(CAP):
        row = out_ref[pl.ds(idx_s[0, k], 1), :]
        for t in range(tiles):
            picked[t, k : k + 1, :] = row[:, t * LANES : (t + 1) * LANES]

    @pl.when(c == 0)
    def _():
        s_id = lax.broadcasted_iota(jnp.int32, (NB, NB), 0)
        block = out_ref[:NB, :].astype(jnp.bfloat16)
        half = NB // CAP
        for h in range(COLS * CAP // NB):
            pick = (slot_row == s_id + h * NB).astype(jnp.float32).astype(jnp.bfloat16)
            sent = jnp.dot(pick, block, preferred_element_type=jnp.float32).astype(jnp.bfloat16)
            tops[h * half : (h + 1) * half] = sent.reshape(half, CAP, cols)

    @pl.when(r == 0)
    def _():
        for k in range(CHUNKS):
            panel[k] = out_ref[k * part : (k + 1) * part, :NB].astype(jnp.bfloat16)

    pl.semaphore_wait(barrier, COLS - 1 + 8)

    def pick_copy(t):
        return pltpu.make_async_remote_copy(
            src_ref=picked.at[t], dst_ref=gathered.at[c], send_sem=sp_send.at[t],
            recv_sem=sp_recv.at[c], device_id=col_dev(owner_of(t)), device_id_type=MESH,
        )

    def for_tiles(body):
        lax.fori_loop(0, tiles, lambda t, _: (body(t), 0)[1], 0)

    @for_tiles
    def _(t):
        @pl.when(owner_of(t) != c)
        def _():
            pick_copy(t).start()

    def pan_copy(k, child, dev):
        return pltpu.make_async_remote_copy(
            src_ref=panel.at[k], dst_ref=panel.at[k], send_sem=pan_send.at[k, child],
            recv_sem=pan_recv.at[k], device_id=dev, device_id_type=MESH,
        )

    def pan_children(k):
        return [
            (r == 0, row_dev(0, 1, 0)),
            (r == 1, row_dev(0, 3, 0)),
            (r == 1, row_dev(1, 0, 0)),
            ((core == 0) & (xlo == 0) & ((y == 1) | (y == 3)), row_dev(1, y, 0)),
            ((core == 0) & (xlo == 0) & (y == (1 if k < CHUNKS // 2 else 3)), row_dev(0, 2, 0)),
            ((core == 0) & (xlo == 1) & (y == 0), row_dev(1, 2, 0)),
            (core == 0, row_dev(xlo, y, 1)),
        ]

    def pan_forward(k):
        for child, (cond, dev) in enumerate(pan_children(k)):
            @pl.when(cond)
            def _():
                pan_copy(k, child, dev).start()

    def pan_wait(k):
        pan_copy(k, 0, row_dev(xlo, y, 1 - core)).wait_recv()

    def top_copy(dst):
        by_hand = dst in RELAYED
        slot_ = RELAYED.index(dst) if by_hand else 0
        return pltpu.make_async_remote_copy(
            src_ref=tops.at[dst], dst_ref=hand.at[slot_] if by_hand else top.at[pl.ds(0, CAP)],
            send_sem=top_send.at[dst], recv_sem=hand_recv.at[slot_] if by_hand else top_recv,
            device_id=col_dev(Z if by_hand else dst), device_id_type=MESH,
        )

    def hand_copy(dst):
        slot_ = RELAYED.index(dst)
        return pltpu.make_async_remote_copy(
            src_ref=hand.at[slot_], dst_ref=top.at[pl.ds(0, CAP)], send_sem=hand_send.at[slot_],
            recv_sem=top_recv, device_id=col_dev(dst), device_id_type=MESH,
        )

    @pl.when(r == 0)
    def _():
        for k in range(CHUNKS):
            pan_forward(k)

    for k in range(CHUNKS):
        @pl.when(c == 0)
        def _():
            for dst in TOP_ORDER[4 * k : 4 * k + 4]:
                top_copy(dst).start()

    @pl.when(c == 0)
    def _():
        pltpu.make_async_copy(tops.at[0], top.at[pl.ds(0, CAP)], own_sem).start()

    @pl.when(r == 1)
    def _():
        for k in range(CHUNKS):
            pan_wait(k)
            pan_forward(k)

    mask[...] = jnp.dot(
        hits[...], jnp.ones((LANES, LANES), jnp.bfloat16), preferred_element_type=jnp.float32
    )

    for h in range(COLS * CAP // NB):
        place = (slot_col == j_id + h * NB).astype(jnp.float32)
        perm[:, h * NB : (h + 1) * NB] = jnp.dot(
            inv_ref[...], place, precision=lax.Precision.HIGHEST, preferred_element_type=jnp.float32
        )

    depth_one = (core == 0) & (((xlo == 0) & ((y == 1) | (y == 3))) | ((xlo == 1) & (y == 0)))

    def z_copy(k):
        return pltpu.make_async_remote_copy(
            src_ref=upper.at[my_tile], dst_ref=upper.at[my_tile], send_sem=z_send.at[DIRECT.index(k)],
            recv_sem=up_recv.at[my_tile], device_id=col_dev(xhi * Z + (z + k) % Z), device_id_type=MESH,
        )

    def x_copy(t):
        return pltpu.make_async_remote_copy(
            src_ref=upper.at[t], dst_ref=upper.at[t], send_sem=x_send.at[t],
            recv_sem=up_recv.at[t], device_id=col_dev((1 - xhi) * Z + z), device_id_type=MESH,
        )

    @pl.when(is_owner)
    def _():
        gathered[c] = picked[my_tile]
        for k in range(1, COLS):
            src = (c + k) % COLS
            pltpu.make_async_remote_copy(
                src_ref=picked.at[0], dst_ref=gathered.at[src], send_sem=sp_send.at[0],
                recv_sem=sp_recv.at[src], device_id=col_dev(src), device_id_type=MESH,
            ).wait_recv()
        solved = jnp.dot(
            perm[...], gathered[...].reshape(COLS * CAP, LANES),
            precision=lax.Precision.HIGHEST, preferred_element_type=jnp.float32,
        )
        upper[my_tile] = solved.astype(jnp.bfloat16)
        for k in DIRECT:
            z_copy(k).start()
        x_copy(my_tile).start()

    def forward_copy(t, sign, to_four):
        half = NB // 2
        which = (1 - sign) // 2
        part_ref = upper.at[t, pl.ds(which * half, half)] if to_four else upper.at[t]
        return pltpu.make_async_remote_copy(
            src_ref=part_ref, dst_ref=part_ref, send_sem=f_send.at[which, int(to_four)],
            recv_sem=half_recv.at[which, t] if to_four else up_recv.at[t],
            device_id=col_dev(xhi * Z + (z + (2 if to_four else 1) * sign + Z) % Z), device_id_type=MESH,
        )

    def ring(away):
        t, owned = tile_of(away)

        @pl.when(owned)
        def _():
            if away == 4:
                forward_copy(t, 1, True).wait_recv()
                forward_copy(t, -1, True).wait_recv()
            else:
                x_copy(t).wait_recv()
            if abs(away) == 2:
                forward_copy(t, -away // 2, False).start()
                forward_copy(t, -away // 2, True).start()
            x_copy(t).start()

    for k in range(max(CHUNKS, len(RELAYED))):
        if k < CHUNKS:
            @pl.when(depth_one)
            def _():
                pan_wait(k)
                pan_forward(k)

        @pl.when(c == Z)
        def _():
            for dst in RELAYED[k : k + 1]:
                top_copy(dst).wait_recv()
                hand_copy(dst).start()

    ring(-2)
    ring(2)

    for away in (-1, 1, -3, 3, 4):
        ring(away)

    @pl.when(jnp.logical_not(depth_one) & (r > 1))
    def _():
        for k in range(CHUNKS):
            pan_wait(k)
            pan_forward(k)

    @pl.when(c == 0)
    def _():
        pltpu.make_async_copy(tops.at[0], top.at[pl.ds(0, CAP)], own_sem).wait()

    @pl.when(c != 0)
    def _():
        top_copy(1).wait_recv()

    first = xhi * RING

    def each_pair(base, body):
        def step(p, _):
            pair = base // 2 + p

            @pl.when((r != 0) | (pair > 0))
            def _():
                body(pair, pl.ds(pl.multiple_of(pair * 2 * LANES, 2 * LANES), 2 * LANES))

            return 0

        lax.fori_loop(0, RING // 2, step, 0)

    def swapped(k, cols_p):
        rows_k = pl.ds(k * part, part)
        moved = jnp.dot(hits[rows_k, :], top[:, cols_p], preferred_element_type=jnp.float32)
        taken = jnp.concatenate([mask[rows_k, :]] * 2, axis=1) > 0.5
        return jnp.where(taken, moved, out_ref[rows_k, cols_p])

    def product(k, solved):
        return jnp.dot(panel[k], solved, preferred_element_type=jnp.float32)

    def finish(solved, cols_p):
        @pl.when(c == 0)
        def _():
            out_ref[:NB, cols_p] = solved.astype(jnp.float32)

    def own_pair(pair, cols_p):
        solved = jnp.concatenate([upper[2 * pair], upper[2 * pair + 1]], axis=1)
        for k in range(CHUNKS):
            out_ref[pl.ds(k * part, part), cols_p] = swapped(k, cols_p) - product(k, solved)
        finish(solved, cols_p)

    def base_pair(pair, cols_p):
        for k in range(CHUNKS):
            out_ref[pl.ds(k * part, part), cols_p] = swapped(k, cols_p)

    def partner_pair(pair, cols_p):
        solved = jnp.concatenate([upper[2 * pair], upper[2 * pair + 1]], axis=1)
        for k in range(CHUNKS):
            rows_k = pl.ds(k * part, part)
            out_ref[rows_k, cols_p] = out_ref[rows_k, cols_p] - product(k, solved)
        finish(solved, cols_p)

    each_pair(first, own_pair)
    each_pair(RING - first, base_pair)
    for q in range(RING // 2):
        pair = (RING - first) // 2 + q
        x_copy(2 * pair).wait_recv()
        x_copy(2 * pair + 1).wait_recv()

        @pl.when((r != 0) | (pair > 0))
        def _():
            partner_pair(pair, pl.ds(pl.multiple_of(pair * 2 * LANES, 2 * LANES), 2 * LANES))

    @for_tiles
    def _(t):
        @pl.when(owner_of(t) != c)
        def _():
            pick_copy(t).wait_send()

    for k in range(CHUNKS):
        for child, (cond, dev) in enumerate(pan_children(k)):
            @pl.when(cond)
            def _():
                pan_copy(k, child, dev).wait_send()

    @pl.when(c == 0)
    def _():
        for dst in range(1, COLS):
            top_copy(dst).wait_send()

    @pl.when(is_owner)
    def _():
        for k in DIRECT:
            z_copy(k).wait_send()

    for away in (-2, 2):
        t, owned = tile_of(away)

        @pl.when(owned)
        def _():
            forward_copy(t, -away // 2, False).wait_send()
            forward_copy(t, -away // 2, True).wait_send()

    @pl.when(c == Z)
    def _():
        for dst in RELAYED:
            hand_copy(dst).wait_send()

    for q in range(RING):
        x_copy(first + q).wait_send()


def store_kernel(src, dst, sems):
    part = src.shape[0] // CHUNKS
    copies = [
        pltpu.make_async_copy(
            src.at[pl.ds(k * part, part)], dst.at[pl.ds(k * part, part)], sems.at[k]
        )
        for k in range(CHUNKS)
    ]
    for copy in copies:
        copy.start()
    for copy in copies:
        copy.wait()


def store(block):
    return pl.pallas_call(
        store_kernel,
        out_shape=jax.ShapeDtypeStruct(block.shape, block.dtype),
        in_specs=[pl.BlockSpec(memory_space=pltpu.VMEM)],
        out_specs=pl.BlockSpec(memory_space=pltpu.HBM),
        scratch_shapes=[pltpu.SemaphoreType.DMA((CHUNKS,))],
        compiler_params=pltpu.CompilerParams(vmem_limit_bytes=1 << 20),
        name="store",
    )(block)


def fast_update(matrix, inverse, pivots):
    rows, cols = matrix.shape
    tiles = cols // LANES
    dma = pltpu.SemaphoreType.DMA
    return pl.pallas_call(
        update_kernel,
        out_shape=(pltpu.VMEM((rows, cols), jnp.float32), jax.ShapeDtypeStruct((1, 1), jnp.int32)),
        in_specs=[
            pl.BlockSpec(memory_space=pltpu.HBM),
            pl.BlockSpec(memory_space=pltpu.VMEM),
            pl.BlockSpec(memory_space=pltpu.VMEM),
        ],
        out_specs=(pl.BlockSpec(memory_space=pltpu.VMEM), pl.BlockSpec(memory_space=pltpu.SMEM)),
        scratch_shapes=[
            pltpu.VMEM((tiles, CAP, LANES), jnp.float32),
            pltpu.VMEM((COLS, CAP, LANES), jnp.float32),
            pltpu.VMEM((CHUNKS, rows // CHUNKS, NB), jnp.bfloat16),
            pltpu.VMEM((tiles, NB, LANES), jnp.bfloat16),
            pltpu.VMEM((COLS, CAP, cols), jnp.bfloat16),
            pltpu.VMEM((LANES, cols), jnp.bfloat16),
            pltpu.VMEM((NB, COLS * CAP), jnp.float32),
            pltpu.VMEM((rows, LANES), jnp.bfloat16),
            pltpu.VMEM((1, LANES), jnp.int32),
            pltpu.SMEM((1, LANES), jnp.int32),
            dma((CHUNKS,)), dma, dma, dma((tiles,)), dma((COLS,)),
            dma((CHUNKS, 7)), dma((CHUNKS,)), dma((COLS,)), dma,
            dma((len(DIRECT),)), dma((2, 2)), dma((tiles,)), dma((tiles,)), dma((2, tiles)),
            pltpu.VMEM((len(RELAYED), CAP, cols), jnp.bfloat16), dma((len(RELAYED),)), dma((len(RELAYED),)),
            pltpu.VMEM((rows, LANES), jnp.float32),
        ],
        compiler_params=pltpu.CompilerParams(
            collective_id=0, has_side_effects=True, vmem_limit_bytes=16 << 20
        ),
        name="update",
    )(matrix, inverse, pivots.reshape(1, NB))


def per_device(matrix, inverse, pivots):
    updated, most = fast_update(matrix, inverse, pivots)
    return lax.cond(
        most[0, 0] < CAP,
        lambda block, *_: block,
        lambda _, *args: any_pivots(*args),
        store(updated), matrix, inverse, pivots,
    )


def solution(mesh):
    return jax.shard_map(
        per_device,
        mesh=mesh,
        in_specs=(P("col", "row"), P(), P()),
        out_specs=P("col", "row"),
        check_vma=False,
    )
```

```python
import functools

import jax
import jax.numpy as jnp
from jax import lax
from jax.experimental import pallas as pl
from jax.experimental.pallas import tpu as pltpu
from jax.sharding import PartitionSpec as P

MESH = pl.DeviceIdType.MESH
NB = 256
CAP = 32
LANES = 128
Z = 8
COLS = 16
CHUNKS = 4
RING = 6
DIRECT = (1, 7, 2, 6)
RELAYED = (12, 11, 10)
TOP_ORDER = (12, 4, 11, 3, 14, 13, 5, 10, 2, 15, 6, 9, 1, 7, 8)


def total(array, axis):
    for step in (1, 2, 4, 8):
        array = array + lax.ppermute(array, axis, [(i, i ^ step) for i in range(COLS)])
    return array


def from_root(array, axis, root):
    mine = lax.axis_index(axis) == root
    return total(jnp.where(mine, array, jnp.zeros_like(array)), axis)


def any_pivots(matrix, inverse, pivots):
    rows_dev, cols_dev = matrix.shape
    block_width = inverse.shape[0]
    grid_col = lax.axis_index("col")
    grid_row = lax.axis_index("row")
    local_rows = pivots - grid_col * rows_dev
    owned_here = (local_rows >= 0) & (local_rows < rows_dev)
    picked = jnp.take(matrix, jnp.clip(local_rows, 0, rows_dev - 1), axis=0)
    picked = jnp.where(owned_here[:, None], picked, 0.0)
    panel_rows = from_root(matrix[:, :block_width].astype(jnp.bfloat16), "row", 0)
    pivot_block = total(picked, "col")
    top_block = from_root(matrix[:block_width].astype(jnp.bfloat16), "col", 0).astype(jnp.float32)
    upper_rows = jnp.dot(
        inverse, pivot_block, precision=lax.Precision.HIGHEST, preferred_element_type=jnp.float32
    )
    row_ids = jnp.arange(rows_dev)
    hit = row_ids[:, None] == local_rows[None, :]
    source = jnp.sum(jnp.where(hit, jnp.arange(block_width)[None, :], 0), axis=1)
    moved = jnp.take(top_block, source, axis=0)
    swapped = jnp.where(jnp.any(hit, axis=1)[:, None], moved, matrix)
    product = jnp.dot(
        panel_rows, upper_rows.astype(jnp.bfloat16), preferred_element_type=jnp.float32
    )
    updated = swapped - product
    solved = jnp.concatenate([upper_rows, jnp.zeros_like(updated[block_width:])], axis=0)
    updated = jnp.where(((grid_col == 0) & (row_ids < block_width))[:, None], solved, updated)
    column_ids = grid_row * cols_dev + jnp.arange(cols_dev)
    return jnp.where((column_ids < block_width)[None, :], matrix, updated)


def update_kernel(
    mat_hbm, inv_ref, piv_ref, out_ref, most_ref,
    picked, gathered, panel, upper, tops, top, perm, hits, idx_v, idx_s,
    load_sem, idx_sem, own_sem, sp_send, sp_recv, pan_send, pan_recv, top_send, top_recv,
    z_send, f_send, x_send, up_recv, half_recv, hand, hand_send, hand_recv, mask,
):
    rows, cols = out_ref.shape
    tiles = cols // LANES
    part = rows // CHUNKS
    r = lax.axis_index("row")
    c = lax.axis_index("col")
    xlo, y, core = r // 8, (r // 2) % 4, r % 2
    xhi, z = c // Z, c % Z

    def row_dev(xlo_, y_, core_):
        return ((xlo_ * 4 + y_) * 2 + core_, c)

    def col_dev(c_):
        return (r, c_)

    def owner_of(t):
        q = t % RING
        return (t // RING) * Z + q + 1 + (q >= 3).astype(jnp.int32)

    def tile_of(away):
        zq = (z + away + Z) % Z
        return xhi * RING + jnp.maximum(zq - 1 - (zq > 4).astype(jnp.int32), 0), zq % 4 != 0

    my_tile, is_owner = tile_of(0)

    loads = [
        pltpu.make_async_copy(
            mat_hbm.at[pl.ds(k * part, part)], out_ref.at[pl.ds(k * part, part)], load_sem.at[k]
        )
        for k in range(CHUNKS)
    ]
    for load in loads:
        load.start()

    barrier = pltpu.get_barrier_semaphore()
    for k in range(1, COLS):
        pl.semaphore_signal(barrier, inc=1, device_id=col_dev((c + k) % COLS), device_id_type=MESH)
    for dev in (
        row_dev(xlo, y, 1 - core), row_dev(xlo, (y + 1) % 4, core),
        row_dev(xlo, (y + 2) % 4, core), row_dev(xlo, (y + 3) % 4, core), row_dev(1 - xlo, y, core),
        row_dev(xlo, (y + 1) % 4, 1 - core), row_dev(xlo, (y + 3) % 4, 1 - core), row_dev(1 - xlo, y, 1 - core),
    ):
        pl.semaphore_signal(barrier, inc=1, device_id=dev, device_id_type=MESH)

    i_id = lax.broadcasted_iota(jnp.int32, (NB, NB), 0)
    j_id = lax.broadcasted_iota(jnp.int32, (NB, NB), 1)
    piv_row = jnp.broadcast_to(piv_ref[...], (NB, NB))
    piv_col = piv_row.T
    own_row, own_col = piv_row // rows, piv_col // rows
    rank = jnp.sum(((own_row == own_col) & (i_id < j_id)).astype(jnp.int32), axis=0, keepdims=True)
    most_ref[0, 0] = jnp.max(rank)
    slot = jnp.where(rank < CAP, own_row[:1] * CAP + rank, -1)
    slot_row = jnp.broadcast_to(slot, (NB, NB))
    slot_col = slot_row.T
    lane = j_id[:, :LANES]
    match = (slot_col[:, :LANES] == c * CAP + lane) & (lane < CAP)
    idx = jnp.sum(
        jnp.where(match, piv_col[:, :LANES] - c * rows + 1, 0), axis=0, keepdims=True
    ) - 1
    idx_v[...] = jnp.maximum(idx, 0)
    idx_copy = pltpu.make_async_copy(idx_v, idx_s, idx_sem)
    idx_copy.start()
    r_id = lax.broadcasted_iota(jnp.int32, (rows, LANES), 0)
    hits[...] = (r_id == jnp.broadcast_to(idx, (rows, LANES))).astype(jnp.float32).astype(jnp.bfloat16)
    top[CAP:, :] = jnp.zeros((LANES - CAP, cols), jnp.bfloat16)
    idx_copy.wait()
    for load in loads:
        load.wait()

    for k in range(CAP):
        row = out_ref[pl.ds(idx_s[0, k], 1), :]
        for t in range(tiles):
            picked[t, k : k + 1, :] = row[:, t * LANES : (t + 1) * LANES]

    @pl.when(c == 0)
    def _():
        s_id = lax.broadcasted_iota(jnp.int32, (NB, NB), 0)
        block = out_ref[:NB, :].astype(jnp.bfloat16)
        half = NB // CAP
        for h in range(COLS * CAP // NB):
            pick = (slot_row == s_id + h * NB).astype(jnp.float32).astype(jnp.bfloat16)
            sent = jnp.dot(pick, block, preferred_element_type=jnp.float32).astype(jnp.bfloat16)
            tops[h * half : (h + 1) * half] = sent.reshape(half, CAP, cols)

    @pl.when(r == 0)
    def _():
        for k in range(CHUNKS):
            panel[k] = out_ref[k * part : (k + 1) * part, :NB].astype(jnp.bfloat16)

    pl.semaphore_wait(barrier, COLS - 1 + 8)

    def pick_copy(t):
        return pltpu.make_async_remote_copy(
            src_ref=picked.at[t], dst_ref=gathered.at[c], send_sem=sp_send.at[t],
            recv_sem=sp_recv.at[c], device_id=col_dev(owner_of(t)), device_id_type=MESH,
        )

    def for_tiles(body):
        lax.fori_loop(0, tiles, lambda t, _: (body(t), 0)[1], 0)

    @for_tiles
    def _(t):
        @pl.when(owner_of(t) != c)
        def _():
            pick_copy(t).start()

    def pan_copy(k, child, dev):
        return pltpu.make_async_remote_copy(
            src_ref=panel.at[k], dst_ref=panel.at[k], send_sem=pan_send.at[k, child],
            recv_sem=pan_recv.at[k], device_id=dev, device_id_type=MESH,
        )

    def pan_children(k):
        return [
            (r == 0, row_dev(0, 1, 0)),
            (r == 1, row_dev(0, 3, 0)),
            (r == 1, row_dev(1, 0, 0)),
            ((core == 0) & (xlo == 0) & ((y == 1) | (y == 3)), row_dev(1, y, 0)),
            ((core == 0) & (xlo == 0) & (y == (1 if k < CHUNKS // 2 else 3)), row_dev(0, 2, 0)),
            ((core == 0) & (xlo == 1) & (y == 0), row_dev(1, 2, 0)),
            (core == 0, row_dev(xlo, y, 1)),
        ]

    def pan_forward(k):
        for child, (cond, dev) in enumerate(pan_children(k)):
            @pl.when(cond)
            def _():
                pan_copy(k, child, dev).start()

    def pan_wait(k):
        pan_copy(k, 0, row_dev(xlo, y, 1 - core)).wait_recv()

    def top_copy(dst):
        by_hand = dst in RELAYED
        slot_ = RELAYED.index(dst) if by_hand else 0
        return pltpu.make_async_remote_copy(
            src_ref=tops.at[dst], dst_ref=hand.at[slot_] if by_hand else top.at[pl.ds(0, CAP)],
            send_sem=top_send.at[dst], recv_sem=hand_recv.at[slot_] if by_hand else top_recv,
            device_id=col_dev(Z if by_hand else dst), device_id_type=MESH,
        )

    def hand_copy(dst):
        slot_ = RELAYED.index(dst)
        return pltpu.make_async_remote_copy(
            src_ref=hand.at[slot_], dst_ref=top.at[pl.ds(0, CAP)], send_sem=hand_send.at[slot_],
            recv_sem=top_recv, device_id=col_dev(dst), device_id_type=MESH,
        )

    @pl.when(r == 0)
    def _():
        for k in range(CHUNKS):
            pan_forward(k)

    for k in range(CHUNKS):
        @pl.when(c == 0)
        def _():
            for dst in TOP_ORDER[4 * k : 4 * k + 4]:
                top_copy(dst).start()

    @pl.when(c == 0)
    def _():
        pltpu.make_async_copy(tops.at[0], top.at[pl.ds(0, CAP)], own_sem).start()

    @pl.when(r == 1)
    def _():
        for k in range(CHUNKS):
            pan_wait(k)
            pan_forward(k)

    mask[...] = jnp.dot(
        hits[...], jnp.ones((LANES, LANES), jnp.bfloat16), preferred_element_type=jnp.float32
    )

    for h in range(COLS * CAP // NB):
        place = (slot_col == j_id + h * NB).astype(jnp.float32)
        perm[:, h * NB : (h + 1) * NB] = jnp.dot(
            inv_ref[...], place, precision=lax.Precision.HIGHEST, preferred_element_type=jnp.float32
        )

    depth_one = (core == 0) & (((xlo == 0) & ((y == 1) | (y == 3))) | ((xlo == 1) & (y == 0)))

    def z_copy(k):
        return pltpu.make_async_remote_copy(
            src_ref=upper.at[my_tile], dst_ref=upper.at[my_tile], send_sem=z_send.at[DIRECT.index(k)],
            recv_sem=up_recv.at[my_tile], device_id=col_dev(xhi * Z + (z + k) % Z), device_id_type=MESH,
        )

    def x_copy(t):
        return pltpu.make_async_remote_copy(
            src_ref=upper.at[t], dst_ref=upper.at[t], send_sem=x_send.at[t],
            recv_sem=up_recv.at[t], device_id=col_dev((1 - xhi) * Z + z), device_id_type=MESH,
        )

    @pl.when(is_owner)
    def _():
        gathered[c] = picked[my_tile]
        for k in range(1, COLS):
            src = (c + k) % COLS
            pltpu.make_async_remote_copy(
                src_ref=picked.at[0], dst_ref=gathered.at[src], send_sem=sp_send.at[0],
                recv_sem=sp_recv.at[src], device_id=col_dev(src), device_id_type=MESH,
            ).wait_recv()
        solved = jnp.dot(
            perm[...], gathered[...].reshape(COLS * CAP, LANES),
            precision=lax.Precision.HIGHEST, preferred_element_type=jnp.float32,
        )
        upper[my_tile] = solved.astype(jnp.bfloat16)
        for k in DIRECT:
            z_copy(k).start()
        x_copy(my_tile).start()

    def forward_copy(t, sign, to_four):
        half = NB // 2
        which = (1 - sign) // 2
        part_ref = upper.at[t, pl.ds(which * half, half)] if to_four else upper.at[t]
        return pltpu.make_async_remote_copy(
            src_ref=part_ref, dst_ref=part_ref, send_sem=f_send.at[which, int(to_four)],
            recv_sem=half_recv.at[which, t] if to_four else up_recv.at[t],
            device_id=col_dev(xhi * Z + (z + (2 if to_four else 1) * sign + Z) % Z), device_id_type=MESH,
        )

    def ring(away):
        t, owned = tile_of(away)

        @pl.when(owned)
        def _():
            if away == 4:
                forward_copy(t, 1, True).wait_recv()
                forward_copy(t, -1, True).wait_recv()
            else:
                x_copy(t).wait_recv()
            if abs(away) == 2:
                forward_copy(t, -away // 2, False).start()
                forward_copy(t, -away // 2, True).start()
            x_copy(t).start()

    for k in range(max(CHUNKS, len(RELAYED))):
        if k < CHUNKS:
            @pl.when(depth_one)
            def _():
                pan_wait(k)
                pan_forward(k)

        @pl.when(c == Z)
        def _():
            for dst in RELAYED[k : k + 1]:
                top_copy(dst).wait_recv()
                hand_copy(dst).start()

    ring(-2)
    ring(2)

    for away in (-1, 1, -3, 3, 4):
        ring(away)

    @pl.when(jnp.logical_not(depth_one) & (r > 1))
    def _():
        for k in range(CHUNKS):
            pan_wait(k)
            pan_forward(k)

    @pl.when(c == 0)
    def _():
        pltpu.make_async_copy(tops.at[0], top.at[pl.ds(0, CAP)], own_sem).wait()

    @pl.when(c != 0)
    def _():
        top_copy(1).wait_recv()

    first = xhi * RING

    def each_pair(base, body):
        def step(p, _):
            pair = base // 2 + p

            @pl.when((r != 0) | (pair > 0))
            def _():
                body(pair, pl.ds(pl.multiple_of(pair * 2 * LANES, 2 * LANES), 2 * LANES))

            return 0

        lax.fori_loop(0, RING // 2, step, 0)

    def swapped(k, cols_p):
        rows_k = pl.ds(k * part, part)
        moved = jnp.dot(hits[rows_k, :], top[:, cols_p], preferred_element_type=jnp.float32)
        taken = jnp.concatenate([mask[rows_k, :]] * 2, axis=1) > 0.5
        return jnp.where(taken, moved, out_ref[rows_k, cols_p])

    def product(k, solved):
        return jnp.dot(panel[k], solved, preferred_element_type=jnp.float32)

    def finish(solved, cols_p):
        @pl.when(c == 0)
        def _():
            out_ref[:NB, cols_p] = solved.astype(jnp.float32)

    def own_pair(pair, cols_p):
        solved = jnp.concatenate([upper[2 * pair], upper[2 * pair + 1]], axis=1)
        for k in range(CHUNKS):
            out_ref[pl.ds(k * part, part), cols_p] = swapped(k, cols_p) - product(k, solved)
        finish(solved, cols_p)

    def base_pair(pair, cols_p):
        for k in range(CHUNKS):
            out_ref[pl.ds(k * part, part), cols_p] = swapped(k, cols_p)

    def partner_pair(pair, cols_p):
        solved = jnp.concatenate([upper[2 * pair], upper[2 * pair + 1]], axis=1)
        for k in range(CHUNKS):
            rows_k = pl.ds(k * part, part)
            out_ref[rows_k, cols_p] = out_ref[rows_k, cols_p] - product(k, solved)
        finish(solved, cols_p)

    each_pair(first, own_pair)
    each_pair(RING - first, base_pair)
    for q in range(RING // 2):
        pair = (RING - first) // 2 + q
        x_copy(2 * pair).wait_recv()
        x_copy(2 * pair + 1).wait_recv()

        @pl.when((r != 0) | (pair > 0))
        def _():
            partner_pair(pair, pl.ds(pl.multiple_of(pair * 2 * LANES, 2 * LANES), 2 * LANES))

    @for_tiles
    def _(t):
        @pl.when(owner_of(t) != c)
        def _():
            pick_copy(t).wait_send()

    for k in range(CHUNKS):
        for child, (cond, dev) in enumerate(pan_children(k)):
            @pl.when(cond)
            def _():
                pan_copy(k, child, dev).wait_send()

    @pl.when(c == 0)
    def _():
        for dst in range(1, COLS):
            top_copy(dst).wait_send()

    @pl.when(is_owner)
    def _():
        for k in DIRECT:
            z_copy(k).wait_send()

    for away in (-2, 2):
        t, owned = tile_of(away)

        @pl.when(owned)
        def _():
            forward_copy(t, -away // 2, False).wait_send()
            forward_copy(t, -away // 2, True).wait_send()

    @pl.when(c == Z)
    def _():
        for dst in RELAYED:
            hand_copy(dst).wait_send()

    for q in range(RING):
        x_copy(first + q).wait_send()


def store_kernel(src, dst, sems):
    part = src.shape[0] // CHUNKS
    copies = [
        pltpu.make_async_copy(
            src.at[pl.ds(k * part, part)], dst.at[pl.ds(k * part, part)], sems.at[k]
        )
        for k in range(CHUNKS)
    ]
    for copy in copies:
        copy.start()
    for copy in copies:
        copy.wait()


def store(block):
    return pl.pallas_call(
        store_kernel,
        out_shape=jax.ShapeDtypeStruct(block.shape, block.dtype),
        in_specs=[pl.BlockSpec(memory_space=pltpu.VMEM)],
        out_specs=pl.BlockSpec(memory_space=pltpu.HBM),
        scratch_shapes=[pltpu.SemaphoreType.DMA((CHUNKS,))],
        compiler_params=pltpu.CompilerParams(vmem_limit_bytes=1 << 20),
        name="store",
    )(block)


def fast_update(matrix, inverse, pivots):
    rows, cols = matrix.shape
    tiles = cols // LANES
    dma = pltpu.SemaphoreType.DMA
    return pl.pallas_call(
        update_kernel,
        out_shape=(pltpu.VMEM((rows, cols), jnp.float32), jax.ShapeDtypeStruct((1, 1), jnp.int32)),
        in_specs=[
            pl.BlockSpec(memory_space=pltpu.HBM),
            pl.BlockSpec(memory_space=pltpu.VMEM),
            pl.BlockSpec(memory_space=pltpu.VMEM),
        ],
        out_specs=(pl.BlockSpec(memory_space=pltpu.VMEM), pl.BlockSpec(memory_space=pltpu.SMEM)),
        scratch_shapes=[
            pltpu.VMEM((tiles, CAP, LANES), jnp.float32),
            pltpu.VMEM((COLS, CAP, LANES), jnp.float32),
            pltpu.VMEM((CHUNKS, rows // CHUNKS, NB), jnp.bfloat16),
            pltpu.VMEM((tiles, NB, LANES), jnp.bfloat16),
            pltpu.VMEM((COLS, CAP, cols), jnp.bfloat16),
            pltpu.VMEM((LANES, cols), jnp.bfloat16),
            pltpu.VMEM((NB, COLS * CAP), jnp.float32),
            pltpu.VMEM((rows, LANES), jnp.bfloat16),
            pltpu.VMEM((1, LANES), jnp.int32),
            pltpu.SMEM((1, LANES), jnp.int32),
            dma((CHUNKS,)), dma, dma, dma((tiles,)), dma((COLS,)),
            dma((CHUNKS, 7)), dma((CHUNKS,)), dma((COLS,)), dma,
            dma((len(DIRECT),)), dma((2, 2)), dma((tiles,)), dma((tiles,)), dma((2, tiles)),
            pltpu.VMEM((len(RELAYED), CAP, cols), jnp.bfloat16), dma((len(RELAYED),)), dma((len(RELAYED),)),
            pltpu.VMEM((rows, LANES), jnp.float32),
        ],
        compiler_params=pltpu.CompilerParams(
            collective_id=0, has_side_effects=True, vmem_limit_bytes=16 << 20
        ),
        name="update",
    )(matrix, inverse, pivots.reshape(1, NB))


def per_device(matrix, inverse, pivots):
    updated, most = fast_update(matrix, inverse, pivots)
    return lax.cond(
        most[0, 0] < CAP,
        lambda block, *_: block,
        lambda _, *args: any_pivots(*args),
        store(updated), matrix, inverse, pivots,
    )


def solution(mesh):
    return jax.shard_map(
        per_device,
        mesh=mesh,
        in_specs=(P("col", "row"), P(), P()),
        out_specs=P("col", "row"),
        check_vma=False,
    )
```
